32 devices in a mesh: ocean: 16 (over z, y, core), sht: 2 (over x).
Axes of the slice: x: 2, y: 2, z: 4, core: 2. Of those that a mesh axis runs over, the one named last changes fastest.
Arguments:
- height: float32 [256, 2048], P('ocean', 'sht'), may hold values from -6 to 6
- east: float32 [256, 2048], P('ocean', 'sht'), may hold values from -3 to 3
- north: float32 [256, 2048], P('ocean', 'sht'), may hold values from -3 to 3
- depth: float32 [256, 2048], P('ocean', 'sht'), may hold values from 0.3 to 1.5
- equilibrium: float32 [256, 2048], P('ocean', 'sht'), may hold values from -3 to 3
- mask: int32 [256, 2048], P('ocean', 'sht'), may hold values from 0 to 1, as said below
- sines: float32 [256], P('ocean'), may hold values from -0.95 to 0.95, as said below
- legendre: float32 [256, 1024, 1024], P('ocean', None, 'sht'), as said below
- love: float32 [1024], replicated, may hold values from 0.01 to 0.3
Outputs:
- level_out: float32 [256, 2048], P('ocean', 'sht')
- east_out: float32 [256, 2048], P('ocean', 'sht')
- north_out: float32 [256, 2048], P('ocean', 'sht')
The draws below stay inside these ranges and needn't reach their ends.
Inputs may be any that keep to these rules, and one draw needn't show every extreme that they name: `mask`: 1 marks ocean, 0 land; rows 0 and 255 and columns 0 and 2047 are land. `sines`: ascending; row j lies within 0.2 / 256 * 1.9 of -0.95 + 1.9 (j + 0.5) / 256. legendre[j, l, m] is the fully normalized associated Legendre function of degree l and order m at sines[j] (unit integral of its square over -1 to 1), zero where l < m.
All inputs are finite; a program needn't handle non-finite values.
Results may differ from the reference program's by a relative error of at most 0.0003.
Values sent between devices are 32-bit elements; how exact they have to be, the bound alone decides.
A program may use at most 128 MiB of HBM per device.

```python
import math
import jax
import jax.numpy as jnp
from jax import lax

NLON = 2048
LDEG = 1024
MORD = 1024
STEPS = 3
NLAT = 256


def row_sines(key):
    jitter = jax.random.uniform(jax.random.fold_in(key, 5), (NLAT,), jnp.float32, -0.2, 0.2)
    placed = (jnp.arange(NLAT, dtype=jnp.float32) + 0.5 + jitter) / NLAT
    return -0.95 + 1.9 * placed


def draw_sines(key, part):
    return row_sines(key)


def draw_legendre(key, part):
    sines = row_sines(key)
    cosine = jnp.sqrt(1.0 - sines * sines)
    order_int = jnp.arange(MORD, dtype=jnp.int32)
    order = order_int.astype(jnp.float32)
    log_steps = jnp.where(order_int > 0, 0.5 * jnp.log((2.0 * order + 1.0) / jnp.maximum(2.0 * order, 1.0)), 0.0)
    log_diag = jnp.log(jnp.sqrt(0.5)) + jnp.cumsum(log_steps)[None, :] + order[None, :] * jnp.log(cosine)[:, None]
    diagonal = jnp.exp(log_diag)
    second = jnp.sqrt(2.0 * order + 3.0)[None, :] * sines[:, None] * diagonal

    def advance(running, degree):
        latest, before = running
        value_l = degree.astype(jnp.float32)
        factor = jnp.sqrt(jnp.maximum(4.0 * value_l * value_l - 1.0, 1.0) / jnp.maximum(value_l * value_l - order * order, 1.0))
        lower = value_l - 1.0
        prior = jnp.sqrt(jnp.maximum(4.0 * lower * lower - 1.0, 1.0) / jnp.maximum(lower * lower - order * order, 1.0))
        general = factor[None, :] * (sines[:, None] * latest - before / prior[None, :])
        value = jnp.where(degree == order_int[None, :], diagonal, jnp.where(degree == order_int[None, :] + 1, second, jnp.where(degree > order_int[None, :] + 1, general, 0.0)))
        return ((value, latest), value)
    zeros = jnp.zeros((NLAT, MORD), jnp.float32)
    _, stacked = lax.scan(advance, (zeros, zeros), jnp.arange(LDEG, dtype=jnp.int32))
    return jnp.transpose(stacked, (1, 0, 2))


def draw_mask(key, part):
    key = jax.random.fold_in(key, 11)
    cells = jax.random.randint(key, (NLAT, NLON), 0, 4)
    row_index = jnp.arange(NLAT, dtype=jnp.int32)[:, None]
    col_index = jnp.arange(NLON, dtype=jnp.int32)[None, :]
    border = (row_index == 0) | (row_index == NLAT - 1) | (col_index == 0) | (col_index == NLON - 1)
    return jnp.where(border | (cells == 0), 0, 1).astype(jnp.int32)


def level_of(rng, dims, pieces, least, top_value):
    def one(dim, parts):
        heights = jax.random.uniform(jax.random.fold_in(jax.random.fold_in(rng, 6), dim), (parts,), jnp.float32, least / len(pieces), top_value / len(pieces))
        return jnp.repeat(jnp.exp(heights), dims[dim] // parts).reshape((-1,) + (1,) * (len(dims) - dim - 1))

    level = one(*pieces[0])
    for cut in pieces[1:]:
        level = level * one(*cut)
    return level


def gaussian(key, dims, deviation, bound, pieces=(), kind=jnp.bfloat16):
    drawn = deviation * jax.random.normal(key, dims, jnp.float32)
    if pieces:
        drawn = drawn * level_of(key, dims, pieces, -0.22, 0.18)
    return jnp.clip(drawn, -bound, bound).astype(kind)


def setup_inputs(seed: int = 0) -> dict:
    streams_of = jax.random.split(jax.random.key(seed), 10)
    return {
        "height": gaussian(streams_of[0], (NLAT, NLON), 1.0, 6.0, ((0, 16), (1, 2)), jnp.float32),
        "east": gaussian(streams_of[1], (NLAT, NLON), 0.5, 3.0, ((0, 16), (1, 2)), jnp.float32),
        "north": gaussian(streams_of[2], (NLAT, NLON), 0.5, 3.0, ((0, 16), (1, 2)), jnp.float32),
        "depth": jnp.clip(0.3 + 1.2 * jax.random.uniform(streams_of[3], (NLAT, NLON), jnp.float32) ** level_of(streams_of[3], (NLAT, NLON), ((0, 16), (1, 2)), -0.2, 0.2), 0.3, 1.5),
        "equilibrium": gaussian(streams_of[4], (NLAT, NLON), 0.5, 3.0, ((0, 16), (1, 2)), jnp.float32),
        "mask": draw_mask(jax.random.fold_in(streams_of[9], 71), 0),
        "sines": draw_sines(jax.random.fold_in(streams_of[9], 71), 0),
        "legendre": draw_legendre(jax.random.fold_in(streams_of[9], 71), 0),
        "love": jnp.clip(jnp.exp(jax.random.uniform(streams_of[8], (LDEG,), jnp.float32, math.log(0.01), math.log(0.3))), 0.01, 0.3),
    }


COURANT = 0.12
ROTATION = 0.5
FRICTION = 0.3
HIGHEST = lax.Precision.HIGHEST

def self_attraction(level, legendre, love):
    lat_total, lon_total = level.shape
    order_total = legendre.shape[2]
    longitude = jnp.arange(lon_total, dtype=jnp.int32)
    order = jnp.arange(order_total, dtype=jnp.int32)
    phase_index = longitude[:, None] * order[None, :] % lon_total
    angles = phase_index.astype(jnp.float32) * (2.0 * math.pi / lon_total)
    analysis = jnp.concatenate([jnp.cos(angles) / lon_total, -jnp.sin(angles) / lon_total], 1)
    spectra = jnp.dot(level, analysis, precision=HIGHEST, preferred_element_type=jnp.float32)
    weighted = spectra.reshape(lat_total, 2, order_total) * (2.0 / lat_total)
    block_width = min(128, order_total)
    block_count = order_total // block_width

    def one_block(block_index):
        table_block = lax.dynamic_slice_in_dim(legendre, block_index * block_width, block_width, 2)
        spectra_block = lax.dynamic_slice_in_dim(weighted, block_index * block_width, block_width, 2)
        coefs = jnp.einsum('jlm,jcm->lcm', table_block, spectra_block, precision=HIGHEST)
        loaded = coefs * love[:, None, None]
        return jnp.einsum('jlm,lcm->jcm', table_block, loaded, precision=HIGHEST)
    blocks = lax.map(one_block, jnp.arange(block_count, dtype=jnp.int32))
    synth = jnp.transpose(blocks, (1, 2, 0, 3)).reshape(lat_total, 2 * order_total)
    doubling = jnp.where(order == 0, 1.0, 2.0).astype(jnp.float32)[:, None]
    turned = jnp.transpose(angles)
    synthesis = jnp.concatenate([jnp.cos(turned) * doubling, -jnp.sin(turned) * doubling], 0)
    return jnp.dot(synth, synthesis, precision=HIGHEST, preferred_element_type=jnp.float32)

def reference(height, east, north, depth, equilibrium, mask, sines, legendre, love):
    wet_cells = mask == 1
    east_coef = (COURANT / jnp.sqrt(1.0 - sines * sines))[:, None]
    coriolis = (ROTATION * sines)[:, None]
    level = jnp.where(wet_cells, height, 0.0)
    eastward, northward = (east, north)
    damping = FRICTION / depth
    for step_index in range(STEPS):
        sal = self_attraction(level, legendre, love)
        potential = level - sal - equilibrium
        padded = jnp.pad(potential, 1)
        grad_east = east_coef * (padded[1:-1, 2:] - padded[1:-1, :-2])
        grad_north = COURANT * (padded[2:, 1:-1] - padded[:-2, 1:-1])
        new_east = jnp.where(wet_cells, eastward + coriolis * northward - grad_east - damping * eastward, 0.0)
        new_north = jnp.where(wet_cells, northward - coriolis * eastward - grad_north - damping * northward, 0.0)
        flux_east = jnp.pad(depth * new_east, 1)
        flux_north = jnp.pad(depth * new_north, 1)
        divergence = east_coef * (flux_east[1:-1, 2:] - flux_east[1:-1, :-2]) + COURANT * (flux_north[2:, 1:-1] - flux_north[:-2, 1:-1])
        level = jnp.where(wet_cells, level - divergence, 0.0)
        eastward, northward = (new_east, new_north)
    return (level, eastward, northward)
```

```python
import functools
import math

import jax
import jax.numpy as jnp
import ml_dtypes
import numpy as np
from jax import lax
from jax.experimental import pallas as pl
from jax.experimental.pallas import tpu as pltpu
from jax.sharding import PartitionSpec as P

STEPS = 3
COURANT = 0.12
ROTATION = 0.5
FRICTION = 0.3
LANES = 128


def fourier_tables(lon_total, order_dev, sht_count):
    k = np.arange(lon_total // 2)[:, None]
    high, low = [], []
    for owner in range(sht_count):
        m = owner * order_dev + np.arange(order_dev)[None, :]
        angle = 2.0 * math.pi * ((k * m) % lon_total) / lon_total
        table = np.concatenate([np.cos(angle), -np.sin(angle)], 1).astype(np.float32)
        top = table.astype(ml_dtypes.bfloat16)
        high.append(top)
        low.append((table - top.astype(np.float32)).astype(ml_dtypes.bfloat16))
    return np.stack(high), np.stack(low)


def split(x):
    top = x.astype(jnp.bfloat16)
    return top, (x - top.astype(jnp.float32)).astype(jnp.bfloat16)


def table_dot(x, high, low, dims):
    rows = x.shape[0]
    top, rest = split(x)
    stacked = jnp.concatenate([top, rest], 0)
    dot = functools.partial(
        lax.dot_general, dimension_numbers=(dims, ((), ())), preferred_element_type=jnp.float32
    )
    main = dot(stacked, high)
    return main[:rows] + main[rows:] + dot(top, low)


def kernel(
    geo,
    height, east, north, depth, equilibrium, mask, sines, love, legendre, table_high, table_low,
    level_out, east_out, north_out,
    leg, high, low, weights, acc, synth,
    pair_send, pair_recv, ring_sum, ring_recv, coefs,
    rows_z, part_out, part_in, pot, flux_e, flux_n,
    halo_top, halo_bottom, halo_left, halo_right,
    load_sem, pair_s, pair_r, ring_s, ring_r, gath_s, gath_r, fwd_s, fwd_r,
    z_s, z_r, sal_s, sal_r, halo_s, halo_r,
):
    rows, cols, order_dev, degrees, sht, ocean = geo
    blocks = order_dev // LANES
    n = ocean // 2
    starts = [0]
    for b in range(blocks):
        starts.append(starts[-1] + degrees - LANES * b)
    chunk = starts[-1] // n
    piece = math.gcd(chunk, LANES)
    pieces = chunk // piece
    lon_total = cols * sht
    lat_total = rows * ocean
    scale = 2.0 / lat_total / lon_total

    o = lax.axis_index("ocean")
    d = lax.axis_index("sht")
    core = lax.rem(o, 2)
    chip = lax.div(o, 2)
    zz, yy = lax.div(chip, 2), lax.rem(chip, 2)
    p = zz * (1 - yy) + (n - 1 - zz) * yy
    back = lax.rem(n - p, n)
    q = p * (1 - core) + back * core
    q_peer = p * core + back * (1 - core)

    def ocean_of(pos):
        far = lax.div(pos, n // 2)
        return 2 * ((1 - far) * 2 * pos + far * (2 * (n - 1 - pos) + 1)) + core

    succ = ocean_of(lax.rem(p + 1 - 2 * core + n, n))
    pred = ocean_of(lax.rem(p - 1 + 2 * core + n, n))
    mate = o + 1 - 2 * core
    below = lax.rem(o + 1, ocean)
    above = lax.rem(o + ocean - 1, ocean)
    right = lax.rem(d + 1, sht)
    left = lax.rem(d + sht - 1, sht)

    loads = []
    for b in range(blocks):
        loads.append(
            pltpu.make_async_copy(
                legendre.at[:, pl.ds(LANES * b, degrees - LANES * b), pl.ds(LANES * b, LANES)],
                leg.at[:, pl.ds(starts[b], degrees - LANES * b), :],
                load_sem.at[b],
            )
        )
    tables = [
        pltpu.make_async_copy(table_high.at[d], high, load_sem.at[blocks]),
        pltpu.make_async_copy(table_low.at[d], low, load_sem.at[blocks + 1]),
    ]
    for copy in tables + loads:
        copy.start()

    barrier = pltpu.get_barrier_semaphore()
    greeted = [{"ocean": i, "sht": d} for i in (succ, pred, mate, below, above)]
    greeted += [{"ocean": o, "sht": lax.rem(d + i, sht)} for i in range(1, sht)]
    for device in greeted:
        pl.semaphore_signal(barrier, inc=1, device_id=device, device_id_type=pl.DeviceIdType.MESH)
    pl.semaphore_wait(barrier, len(greeted))

    def remote(src, dst, send, recv, ocean_to, sht_to):
        return pltpu.make_async_remote_copy(
            src_ref=src,
            dst_ref=dst,
            send_sem=send,
            recv_sem=recv,
            device_id={"ocean": ocean_to, "sht": sht_to},
            device_id_type=pl.DeviceIdType.MESH,
        )

    def ring_copy(s):
        return remote(ring_sum.at[s], ring_recv.at[s], ring_s.at[s], ring_r.at[s], succ, d)

    def pair_copy(s):
        return remote(pair_send.at[s], pair_recv.at[s], pair_s.at[s], pair_r.at[s], mate, d)

    def gather_copy(s):
        at = coefs.at[core, lax.rem(q + 1 - s + n, n)]
        return remote(at, at, gath_s.at[s], gath_r.at[s], succ, d)

    def forward_copy(s):
        at = coefs.at[core, lax.rem(q + 1 - s + n, n)]
        return remote(at, at, fwd_s.at[s], fwd_r.at[s], mate, d)

    def block_of(row):
        b = 0
        for at in starts[1:-1]:
            b = b + (row >= at).astype(jnp.int32)
        return b

    def analyse(c, which, dst):
        @pl.loop(0, pieces)
        def _(i):
            row = which * chunk + i * piece
            b = block_of(row)
            w = [weights[c, b, j] for j in range(rows)]
            for tile in range(piece // 8):
                at = pl.ds(pl.multiple_of(row + tile * 8, 8), 8)
                terms = [leg[j, at, :] * w[j] for j in range(rows)]
                while len(terms) > 1:
                    terms = [x + y for x, y in zip(terms[::2], terms[1::2])]
                dst[pl.ds(pl.multiple_of(i * piece + tile * 8, 8), 8), :] = terms[0]

    def synthesise(c, which):
        @pl.loop(0, pieces)
        def _(i):
            row = which * chunk + i * piece
            b = block_of(row)
            sums = [acc[c, b, j] for j in range(rows)]
            for tile in range(piece // 8):
                at = pl.ds(pl.multiple_of(row + tile * 8, 8), 8)
                x = coefs[c, which, pl.ds(pl.multiple_of(i * piece + tile * 8, 8), 8), :]
                sums = [sums[j] + leg[j, at, :] * x for j in range(rows)]
            for j in range(rows):
                acc[c, b, j] = sums[j]

    lane = lax.broadcasted_iota(jnp.int32, (rows, cols), 1)
    row_id = lax.broadcasted_iota(jnp.int32, (rows, cols), 0)
    order_lane = lax.rem(lax.broadcasted_iota(jnp.int32, (rows, 2 * order_dev), 1), order_dev)
    even = lax.rem(order_lane, 2) == 0
    doubling = jnp.where(order_lane + d * order_dev == 0, 1.0, 2.0)

    def shifted(x, axis, forward, edge):
        size = x.shape[axis]
        place = (row_id, lane)[axis]
        if forward:
            return jnp.where(place == size - 1, edge, pltpu.roll(x, size - 1, axis))
        return jnp.where(place == 0, edge, pltpu.roll(x, 1, axis))

    sine = sines[...]
    east_coef = COURANT / jnp.sqrt(1.0 - sine * sine)
    coriolis = ROTATION * sine

    level_out[...] = jnp.where(mask[...] == 1, height[...], 0.0)
    east_out[...] = east[...]
    north_out[...] = north[...]
    for copy in tables:
        copy.wait()

    @pl.loop(0, STEPS)
    def _(step):
        rows_z[d] = level_out[...]
        z_copies = [
            remote(rows_z.at[d], rows_z.at[d], z_s.at[i], z_r.at[i], o, lax.rem(d + i, sht))
            for i in range(1, sht)
        ]
        for copy in z_copies:
            copy.start()
        for copy in z_copies:
            copy.wait()
        first = [rows_z[i] for i in range(sht // 2)]
        second = [rows_z[i + sht // 2] for i in range(sht // 2)]
        plus = jnp.concatenate([x + y for x, y in zip(first, second)], 1)
        minus = jnp.concatenate([x - y for x, y in zip(first, second)], 1)
        sums = table_dot(
            jnp.concatenate([plus, minus], 0), high[...], low[...], (((1,), (0,)))
        )
        spectra = jnp.where(even, sums[:rows], sums[rows:]) * scale
        for c in range(2):
            for b in range(blocks):
                at = c * order_dev + b * LANES
                for j in range(rows):
                    weights[c, b, j] = jnp.broadcast_to(
                        spectra[j : j + 1, at : at + LANES], (8, LANES)
                    )
        acc[...] = jnp.zeros_like(acc)

        @pl.when(step == 0)
        def _():
            for copy in loads:
                copy.wait()

        @pl.loop(0, n)
        def _(s):
            analyse(1 - core, lax.rem(q_peer - s + n, n), pair_send.at[s])
            pair_copy(s).start()
            analyse(core, lax.rem(q - s + n, n), ring_sum.at[s])
            pair_copy(s).wait_recv()
            ring_sum[s] = ring_sum[s] + pair_recv[s]

            @pl.when(s > 0)
            def _():
                ring_copy(s - 1).wait_recv()
                ring_sum[s] = ring_sum[s] + ring_recv[s - 1]

            @pl.when(s < n - 1)
            def _():
                ring_copy(s).start()

        coefs[core, lax.rem(q + 1, n)] = ring_sum[n - 1] * love[...]

        @pl.loop(0, n)
        def _(s):
            @pl.when(s > 0)
            def _():
                gather_copy(s - 1).wait_recv()

            @pl.when(s < n - 1)
            def _():
                gather_copy(s).start()

            forward_copy(s).start()
            synthesise(core, lax.rem(q + 1 - s + n, n))
            forward_copy(s).wait_recv()
            synthesise(1 - core, lax.rem(q_peer + 1 - s + n, n))

        @pl.loop(0, n)
        def _(s):
            pair_copy(s).wait_send()
            forward_copy(s).wait_send()

            @pl.when(s < n - 1)
            def _():
                ring_copy(s).wait_send()
                gather_copy(s).wait_send()

        for c in range(2):
            for b in range(blocks):
                at = c * order_dev + b * LANES
                synth[:, at : at + LANES] = jnp.sum(acc[c, b], axis=1)
        y = synth[...] * doubling
        halves = table_dot(
            jnp.concatenate([jnp.where(even, y, 0.0), jnp.where(even, 0.0, y)], 0),
            high[...], low[...], (((1,), (1,))),
        )
        both = (halves[:rows] + halves[rows:], halves[:rows] - halves[rows:])
        for i in range(sht):
            at = (i % (sht // 2)) * cols
            part_out[i] = both[i // (sht // 2)][:, at : at + cols]
        part_in[d] = part_out[d]
        sal_copies = []
        for i in range(1, sht):
            to = lax.rem(d + i, sht)
            sal_copies.append(
                remote(part_out.at[to], part_in.at[d], sal_s.at[i], sal_r.at[i], o, to)
            )
        for copy in sal_copies:
            copy.start()
        for copy in sal_copies:
            copy.wait()
        sal = part_in[0]
        for i in range(1, sht):
            sal = sal + part_in[i]

        wet = mask[...] == 1
        pot[...] = level_out[...] - sal - equilibrium[...]
        copies = [
            remote(pot.at[pl.ds(rows - 8, 8)], halo_top.at[0], halo_s.at[0], halo_r.at[0], below, d),
            remote(pot.at[pl.ds(0, 8)], halo_bottom.at[0], halo_s.at[1], halo_r.at[1], above, d),
            remote(
                pot.at[:, pl.ds(cols - LANES, LANES)], halo_left.at[0],
                halo_s.at[2], halo_r.at[2], o, right,
            ),
            remote(
                pot.at[:, pl.ds(0, LANES)], halo_right.at[0],
                halo_s.at[3], halo_r.at[3], o, left,
            ),
        ]
        for copy in copies:
            copy.start()
        for copy in copies:
            copy.wait()
        here = pot[...]
        grad_east = east_coef * (
            shifted(here, 1, True, halo_right[0][:, :1])
            - shifted(here, 1, False, halo_left[0][:, LANES - 1 :])
        )
        grad_north = COURANT * (
            shifted(here, 0, True, halo_bottom[0][:1, :])
            - shifted(here, 0, False, halo_top[0][7:, :])
        )
        old_east, old_north = east_out[...], north_out[...]
        deep = depth[...]
        damping = FRICTION / deep
        new_east = jnp.where(
            wet, old_east + coriolis * old_north - grad_east - damping * old_east, 0.0
        )
        new_north = jnp.where(
            wet, old_north - coriolis * old_east - grad_north - damping * old_north, 0.0
        )
        east_out[...] = new_east
        north_out[...] = new_north
        flux_e[...] = deep * new_east
        flux_n[...] = deep * new_north
        copies = [
            remote(
                flux_n.at[pl.ds(rows - 8, 8)], halo_top.at[1], halo_s.at[4], halo_r.at[4], below, d
            ),
            remote(flux_n.at[pl.ds(0, 8)], halo_bottom.at[1], halo_s.at[5], halo_r.at[5], above, d),
            remote(
                flux_e.at[:, pl.ds(cols - LANES, LANES)], halo_left.at[1],
                halo_s.at[6], halo_r.at[6], o, right,
            ),
            remote(
                flux_e.at[:, pl.ds(0, LANES)], halo_right.at[1],
                halo_s.at[7], halo_r.at[7], o, left,
            ),
        ]
        for copy in copies:
            copy.start()
        for copy in copies:
            copy.wait()
        fe, fn = flux_e[...], flux_n[...]
        divergence = east_coef * (
            shifted(fe, 1, True, halo_right[1][:, :1])
            - shifted(fe, 1, False, halo_left[1][:, LANES - 1 :])
        ) + COURANT * (
            shifted(fn, 0, True, halo_bottom[1][:1, :])
            - shifted(fn, 0, False, halo_top[1][7:, :])
        )
        level_out[...] = jnp.where(wet, level_out[...] - divergence, 0.0)


def per_device(height, east, north, depth, equilibrium, mask, sines, legendre, love):
    rows, cols = height.shape
    degrees, order_dev = legendre.shape[1:]
    sht = lax.axis_size("sht")
    ocean = lax.axis_size("ocean")
    blocks = order_dev // LANES
    n = ocean // 2
    packed = sum(degrees - LANES * b for b in range(blocks))
    chunk = packed // n
    high, low = fourier_tables(cols * sht, order_dev, sht)

    o = lax.axis_index("ocean")
    core, chip = o % 2, o // 2
    p = jnp.where(chip % 2 == 0, chip // 2, n - 1 - chip // 2)
    q = jnp.where(core == 0, p, (n - p) % n)
    packed_love = jnp.concatenate([love[LANES * b :] for b in range(blocks)])
    own_love = lax.dynamic_slice(packed_love, (((q + 1) % n) * chunk,), (chunk,))
    own_love = jnp.broadcast_to(own_love[:, None], (chunk, LANES))

    f32 = jnp.float32
    vmem = pl.BlockSpec(memory_space=pltpu.VMEM)
    hbm = pl.BlockSpec(memory_space=pl.ANY)
    dma = lambda k: pltpu.SemaphoreType.DMA((k,))
    half = cols * sht // 2
    grid = jax.ShapeDtypeStruct((rows, cols), f32)
    return pl.pallas_call(
        functools.partial(kernel, (rows, cols, order_dev, degrees, sht, ocean)),
        out_shape=(grid, grid, grid),
        in_specs=[vmem] * 8 + [hbm] * 3,
        out_specs=(vmem, vmem, vmem),
        scratch_shapes=[
            pltpu.VMEM((rows, packed, LANES), f32),
            pltpu.VMEM((half, 2 * order_dev), jnp.bfloat16),
            pltpu.VMEM((half, 2 * order_dev), jnp.bfloat16),
            pltpu.VMEM((2, blocks, rows, 8, LANES), f32),
            pltpu.VMEM((2, blocks, rows, 8, LANES), f32),
            pltpu.VMEM((rows, 2 * order_dev), f32),
            pltpu.VMEM((n, chunk, LANES), f32),
            pltpu.VMEM((n, chunk, LANES), f32),
            pltpu.VMEM((n, chunk, LANES), f32),
            pltpu.VMEM((n, chunk, LANES), f32),
            pltpu.VMEM((2, n, chunk, LANES), f32),
            pltpu.VMEM((sht, rows, cols), f32),
            pltpu.VMEM((sht, rows, cols), f32),
            pltpu.VMEM((sht, rows, cols), f32),
            pltpu.VMEM((rows, cols), f32),
            pltpu.VMEM((rows, cols), f32),
            pltpu.VMEM((rows, cols), f32),
            pltpu.VMEM((2, 8, cols), f32),
            pltpu.VMEM((2, 8, cols), f32),
            pltpu.VMEM((2, rows, LANES), f32),
            pltpu.VMEM((2, rows, LANES), f32),
            dma(blocks + 2),
            dma(n), dma(n), dma(n), dma(n), dma(n), dma(n), dma(n), dma(n),
            dma(sht), dma(sht), dma(sht), dma(sht), dma(8), dma(8),
        ],
        compiler_params=pltpu.CompilerParams(
            collective_id=0, has_side_effects=True, vmem_limit_bytes=60 * 1024 * 1024
        ),
    )(
        height, east, north, depth, equilibrium, mask, sines[:, None], own_love, legendre,
        jnp.asarray(high), jnp.asarray(low),
    )


def solution(mesh):
    grid = P("ocean", "sht")
    in_specs = (grid,) * 6 + (P("ocean"), P("ocean", None, "sht"), P())
    return jax.shard_map(
        per_device, mesh=mesh, in_specs=in_specs, out_specs=(grid,) * 3, check_vma=False
    )
```

```python
import functools
import math

import jax
import jax.numpy as jnp
import ml_dtypes
import numpy as np
from jax import lax
from jax.experimental import pallas as pl
from jax.experimental.pallas import tpu as pltpu
from jax.sharding import PartitionSpec as P

STEPS = 3
COURANT = 0.12
ROTATION = 0.5
FRICTION = 0.3
LANES = 128


def fourier_tables(lon_total, order_dev, sht_count):
    k = np.arange(lon_total // 2)[:, None]
    high, low = [], []
    for owner in range(sht_count):
        m = owner * order_dev + np.arange(order_dev)[None, :]
        angle = 2.0 * math.pi * ((k * m) % lon_total) / lon_total
        table = np.concatenate([np.cos(angle), -np.sin(angle)], 1).astype(np.float32)
        top = table.astype(ml_dtypes.bfloat16)
        high.append(top)
        low.append((table - top.astype(np.float32)).astype(ml_dtypes.bfloat16))
    return np.stack(high), np.stack(low)


def split(x):
    top = x.astype(jnp.bfloat16)
    return top, (x - top.astype(jnp.float32)).astype(jnp.bfloat16)


def table_dot(x, high, low, dims):
    rows = x.shape[0]
    top, rest = split(x)
    stacked = jnp.concatenate([top, rest], 0)
    dot = functools.partial(
        lax.dot_general, dimension_numbers=(dims, ((), ())), preferred_element_type=jnp.float32
    )
    main = dot(stacked, high)
    return main[:rows] + main[rows:] + dot(top, low)


def kernel(
    geo,
    height, east, north, depth, equilibrium, mask, sines, love, legendre, table_high, table_low,
    level_out, east_out, north_out,
    leg, high, low, weights, acc, synth,
    pair_send, pair_recv, ring_sum, ring_recv, coefs,
    rows_z, part_out, part_in, pot, flux_e, flux_n,
    halo_top, halo_bottom, halo_left, halo_right,
    load_sem, pair_s, pair_r, ring_s, ring_r, gath_s, gath_r, fwd_s, fwd_r,
    z_s, z_r, sal_s, sal_r, halo_s, halo_r,
):
    rows, cols, order_dev, degrees, sht, ocean = geo
    blocks = order_dev // LANES
    n = ocean // 2
    starts = [0]
    for b in range(blocks):
        starts.append(starts[-1] + degrees - LANES * b)
    chunk = starts[-1] // n
    piece = math.gcd(chunk, 32)
    pieces = chunk // piece
    cut = (pieces + 1) // 2
    spans = ((0, cut), (cut, pieces))
    lon_total = cols * sht
    lat_total = rows * ocean
    scale = 2.0 / lat_total / lon_total

    o = lax.axis_index("ocean")
    d = lax.axis_index("sht")
    core = lax.rem(o, 2)
    chip = lax.div(o, 2)
    zz, yy = lax.div(chip, 2), lax.rem(chip, 2)
    p = zz * (1 - yy) + (n - 1 - zz) * yy
    back = lax.rem(n - p, n)
    q = p * (1 - core) + back * core
    q_peer = p * core + back * (1 - core)

    def ocean_of(pos):
        far = lax.div(pos, n // 2)
        return 2 * ((1 - far) * 2 * pos + far * (2 * (n - 1 - pos) + 1)) + core

    succ = ocean_of(lax.rem(p + 1 - 2 * core + n, n))
    pred = ocean_of(lax.rem(p - 1 + 2 * core + n, n))
    mate = o + 1 - 2 * core
    below = lax.rem(o + 1, ocean)
    above = lax.rem(o + ocean - 1, ocean)
    right = lax.rem(d + 1, sht)
    left = lax.rem(d + sht - 1, sht)

    loads = []
    for b in range(blocks):
        loads.append(
            pltpu.make_async_copy(
                legendre.at[:, pl.ds(LANES * b, degrees - LANES * b), pl.ds(LANES * b, LANES)],
                leg.at[:, pl.ds(starts[b], degrees - LANES * b), :],
                load_sem.at[b],
            )
        )
    tables = [
        pltpu.make_async_copy(table_high.at[d], high, load_sem.at[blocks]),
        pltpu.make_async_copy(table_low.at[d], low, load_sem.at[blocks + 1]),
    ]
    for copy in tables + loads:
        copy.start()

    barrier = pltpu.get_barrier_semaphore()
    greeted = [{"ocean": i, "sht": d} for i in (succ, pred, mate, below, above)]
    greeted += [{"ocean": o, "sht": lax.rem(d + i, sht)} for i in range(1, sht)]
    for device in greeted:
        pl.semaphore_signal(barrier, inc=1, device_id=device, device_id_type=pl.DeviceIdType.MESH)
    pl.semaphore_wait(barrier, len(greeted))

    def remote(src, dst, send, recv, ocean_to, sht_to):
        return pltpu.make_async_remote_copy(
            src_ref=src,
            dst_ref=dst,
            send_sem=send,
            recv_sem=recv,
            device_id={"ocean": ocean_to, "sht": sht_to},
            device_id_type=pl.DeviceIdType.MESH,
        )

    def part(h):
        return pl.ds(spans[h][0] * piece, (spans[h][1] - spans[h][0]) * piece)

    def ring_copy(s, h):
        src, dst = ring_sum.at[s, part(h), :], ring_recv.at[s, part(h), :]
        return remote(src, dst, ring_s.at[h, s], ring_r.at[h, s], succ, d)

    def pair_copy(s, h):
        src, dst = pair_send.at[s, part(h), :], pair_recv.at[s, part(h), :]
        return remote(src, dst, pair_s.at[h, s], pair_r.at[h, s], mate, d)

    def gather_copy(s, h):
        at = coefs.at[core, lax.rem(q + 1 - s + n, n), part(h), :]
        return remote(at, at, gath_s.at[h, s], gath_r.at[h, s], succ, d)

    def forward_copy(s, h):
        at = coefs.at[core, lax.rem(q + 1 - s + n, n), part(h), :]
        return remote(at, at, fwd_s.at[h, s], fwd_r.at[h, s], mate, d)

    def block_of(row):
        b = 0
        for at in starts[1:-1]:
            b = b + (row >= at).astype(jnp.int32)
        return b

    def analyse(c, which, dst, h):
        @pl.loop(*spans[h])
        def _(i):
            row = which * chunk + i * piece
            b = block_of(row)
            w = [weights[c, b, j] for j in range(rows)]
            for tile in range(piece // 8):
                at = pl.ds(pl.multiple_of(row + tile * 8, 8), 8)
                terms = [leg[j, at, :] * w[j] for j in range(rows)]
                while len(terms) > 1:
                    terms = [x + y for x, y in zip(terms[::2], terms[1::2])]
                dst[pl.ds(pl.multiple_of(i * piece + tile * 8, 8), 8), :] = terms[0]

    def synthesise(c, which, h):
        @pl.loop(*spans[h])
        def _(i):
            row = which * chunk + i * piece
            b = block_of(row)
            sums = [acc[c, b, j] for j in range(rows)]
            for tile in range(piece // 8):
                at = pl.ds(pl.multiple_of(row + tile * 8, 8), 8)
                x = coefs[c, which, pl.ds(pl.multiple_of(i * piece + tile * 8, 8), 8), :]
                sums = [sums[j] + leg[j, at, :] * x for j in range(rows)]
            for j in range(rows):
                acc[c, b, j] = sums[j]

    lane = lax.broadcasted_iota(jnp.int32, (rows, cols), 1)
    row_id = lax.broadcasted_iota(jnp.int32, (rows, cols), 0)
    order_lane = lax.rem(lax.broadcasted_iota(jnp.int32, (rows, 2 * order_dev), 1), order_dev)
    even = lax.rem(order_lane, 2) == 0
    doubling = jnp.where(order_lane + d * order_dev == 0, 1.0, 2.0)

    def shifted(x, axis, forward, edge):
        size = x.shape[axis]
        place = (row_id, lane)[axis]
        if forward:
            return jnp.where(place == size - 1, edge, pltpu.roll(x, size - 1, axis))
        return jnp.where(place == 0, edge, pltpu.roll(x, 1, axis))

    sine = sines[...]
    east_coef = COURANT / jnp.sqrt(1.0 - sine * sine)
    coriolis = ROTATION * sine

    level_out[...] = jnp.where(mask[...] == 1, height[...], 0.0)
    east_out[...] = east[...]
    north_out[...] = north[...]
    for copy in tables:
        copy.wait()

    @pl.loop(0, STEPS)
    def _(step):
        rows_z[d] = level_out[...]
        z_copies = [
            remote(rows_z.at[d], rows_z.at[d], z_s.at[i], z_r.at[i], o, lax.rem(d + i, sht))
            for i in range(1, sht)
        ]
        for copy in z_copies:
            copy.start()
        for copy in z_copies:
            copy.wait()
        first = [rows_z[i] for i in range(sht // 2)]
        second = [rows_z[i + sht // 2] for i in range(sht // 2)]
        plus = jnp.concatenate([x + y for x, y in zip(first, second)], 1)
        minus = jnp.concatenate([x - y for x, y in zip(first, second)], 1)
        sums = table_dot(
            jnp.concatenate([plus, minus], 0), high[...], low[...], (((1,), (0,)))
        )
        spectra = jnp.where(even, sums[:rows], sums[rows:]) * scale
        for c in range(2):
            for b in range(blocks):
                at = c * order_dev + b * LANES
                for j in range(rows):
                    weights[c, b, j] = jnp.broadcast_to(
                        spectra[j : j + 1, at : at + LANES], (8, LANES)
                    )
        acc[...] = jnp.zeros_like(acc)

        @pl.when(step == 0)
        def _():
            for copy in loads:
                copy.wait()

        @pl.loop(0, n)
        def _(s):
            for h in range(2):
                analyse(1 - core, lax.rem(q_peer - s + n, n), pair_send.at[s], h)
                pair_copy(s, h).start()
                analyse(core, lax.rem(q - s + n, n), ring_sum.at[s], h)
                pair_copy(s, h).wait_recv()
                ring_sum[s, part(h), :] = ring_sum[s, part(h), :] + pair_recv[s, part(h), :]

                @pl.when(s > 0)
                def _():
                    ring_copy(s - 1, h).wait_recv()
                    ring_sum[s, part(h), :] = (
                        ring_sum[s, part(h), :] + ring_recv[s - 1, part(h), :]
                    )

                @pl.when(s < n - 1)
                def _():
                    ring_copy(s, h).start()

        coefs[core, lax.rem(q + 1, n)] = ring_sum[n - 1] * love[...]

        @pl.loop(0, n)
        def _(s):
            for h in range(2):

                @pl.when(s > 0)
                def _():
                    gather_copy(s - 1, h).wait_recv()

                @pl.when(s < n - 1)
                def _():
                    gather_copy(s, h).start()

                forward_copy(s, h).start()
                synthesise(core, lax.rem(q + 1 - s + n, n), h)
                forward_copy(s, h).wait_recv()
                synthesise(1 - core, lax.rem(q_peer + 1 - s + n, n), h)

        @pl.loop(0, n)
        def _(s):
            for h in range(2):
                pair_copy(s, h).wait_send()
                forward_copy(s, h).wait_send()

                @pl.when(s < n - 1)
                def _():
                    ring_copy(s, h).wait_send()
                    gather_copy(s, h).wait_send()

        for c in range(2):
            for b in range(blocks):
                at = c * order_dev + b * LANES
                synth[:, at : at + LANES] = jnp.sum(acc[c, b], axis=1)
        y = synth[...] * doubling
        halves = table_dot(
            jnp.concatenate([jnp.where(even, y, 0.0), jnp.where(even, 0.0, y)], 0),
            high[...], low[...], (((1,), (1,))),
        )
        both = (halves[:rows] + halves[rows:], halves[:rows] - halves[rows:])
        for i in range(sht):
            at = (i % (sht // 2)) * cols
            part_out[i] = both[i // (sht // 2)][:, at : at + cols]
        part_in[d] = part_out[d]
        sal_copies = []
        for i in range(1, sht):
            to = lax.rem(d + i, sht)
            sal_copies.append(
                remote(part_out.at[to], part_in.at[d], sal_s.at[i], sal_r.at[i], o, to)
            )
        for copy in sal_copies:
            copy.start()
        for copy in sal_copies:
            copy.wait()
        sal = part_in[0]
        for i in range(1, sht):
            sal = sal + part_in[i]

        wet = mask[...] == 1
        pot[...] = level_out[...] - sal - equilibrium[...]
        copies = [
            remote(pot.at[pl.ds(rows - 8, 8)], halo_top.at[0], halo_s.at[0], halo_r.at[0], below, d),
            remote(pot.at[pl.ds(0, 8)], halo_bottom.at[0], halo_s.at[1], halo_r.at[1], above, d),
            remote(
                pot.at[:, pl.ds(cols - LANES, LANES)], halo_left.at[0],
                halo_s.at[2], halo_r.at[2], o, right,
            ),
            remote(
                pot.at[:, pl.ds(0, LANES)], halo_right.at[0],
                halo_s.at[3], halo_r.at[3], o, left,
            ),
        ]
        for copy in copies:
            copy.start()
        for copy in copies:
            copy.wait()
        here = pot[...]
        grad_east = east_coef * (
            shifted(here, 1, True, halo_right[0][:, :1])
            - shifted(here, 1, False, halo_left[0][:, LANES - 1 :])
        )
        grad_north = COURANT * (
            shifted(here, 0, True, halo_bottom[0][:1, :])
            - shifted(here, 0, False, halo_top[0][7:, :])
        )
        old_east, old_north = east_out[...], north_out[...]
        deep = depth[...]
        damping = FRICTION / deep
        new_east = jnp.where(
            wet, old_east + coriolis * old_north - grad_east - damping * old_east, 0.0
        )
        new_north = jnp.where(
            wet, old_north - coriolis * old_east - grad_north - damping * old_north, 0.0
        )
        east_out[...] = new_east
        north_out[...] = new_north
        flux_e[...] = deep * new_east
        flux_n[...] = deep * new_north
        copies = [
            remote(
                flux_n.at[pl.ds(rows - 8, 8)], halo_top.at[1], halo_s.at[4], halo_r.at[4], below, d
            ),
            remote(flux_n.at[pl.ds(0, 8)], halo_bottom.at[1], halo_s.at[5], halo_r.at[5], above, d),
            remote(
                flux_e.at[:, pl.ds(cols - LANES, LANES)], halo_left.at[1],
                halo_s.at[6], halo_r.at[6], o, right,
            ),
            remote(
                flux_e.at[:, pl.ds(0, LANES)], halo_right.at[1],
                halo_s.at[7], halo_r.at[7], o, left,
            ),
        ]
        for copy in copies:
            copy.start()
        for copy in copies:
            copy.wait()
        fe, fn = flux_e[...], flux_n[...]
        divergence = east_coef * (
            shifted(fe, 1, True, halo_right[1][:, :1])
            - shifted(fe, 1, False, halo_left[1][:, LANES - 1 :])
        ) + COURANT * (
            shifted(fn, 0, True, halo_bottom[1][:1, :])
            - shifted(fn, 0, False, halo_top[1][7:, :])
        )
        level_out[...] = jnp.where(wet, level_out[...] - divergence, 0.0)


def per_device(height, east, north, depth, equilibrium, mask, sines, legendre, love):
    rows, cols = height.shape
    degrees, order_dev = legendre.shape[1:]
    sht = lax.axis_size("sht")
    ocean = lax.axis_size("ocean")
    blocks = order_dev // LANES
    n = ocean // 2
    packed = sum(degrees - LANES * b for b in range(blocks))
    chunk = packed // n
    high, low = fourier_tables(cols * sht, order_dev, sht)

    o = lax.axis_index("ocean")
    core, chip = o % 2, o // 2
    p = jnp.where(chip % 2 == 0, chip // 2, n - 1 - chip // 2)
    q = jnp.where(core == 0, p, (n - p) % n)
    packed_love = jnp.concatenate([love[LANES * b :] for b in range(blocks)])
    own_love = lax.dynamic_slice(packed_love, (((q + 1) % n) * chunk,), (chunk,))
    own_love = jnp.broadcast_to(own_love[:, None], (chunk, LANES))

    f32 = jnp.float32
    vmem = pl.BlockSpec(memory_space=pltpu.VMEM)
    hbm = pl.BlockSpec(memory_space=pl.ANY)
    dma = lambda k: pltpu.SemaphoreType.DMA((k,))
    half = cols * sht // 2
    grid = jax.ShapeDtypeStruct((rows, cols), f32)
    return pl.pallas_call(
        functools.partial(kernel, (rows, cols, order_dev, degrees, sht, ocean)),
        out_shape=(grid, grid, grid),
        in_specs=[vmem] * 8 + [hbm] * 3,
        out_specs=(vmem, vmem, vmem),
        scratch_shapes=[
            pltpu.VMEM((rows, packed, LANES), f32),
            pltpu.VMEM((half, 2 * order_dev), jnp.bfloat16),
            pltpu.VMEM((half, 2 * order_dev), jnp.bfloat16),
            pltpu.VMEM((2, blocks, rows, 8, LANES), f32),
            pltpu.VMEM((2, blocks, rows, 8, LANES), f32),
            pltpu.VMEM((rows, 2 * order_dev), f32),
            pltpu.VMEM((n, chunk, LANES), f32),
            pltpu.VMEM((n, chunk, LANES), f32),
            pltpu.VMEM((n, chunk, LANES), f32),
            pltpu.VMEM((n, chunk, LANES), f32),
            pltpu.VMEM((2, n, chunk, LANES), f32),
            pltpu.VMEM((sht, rows, cols), f32),
            pltpu.VMEM((sht, rows, cols), f32),
            pltpu.VMEM((sht, rows, cols), f32),
            pltpu.VMEM((rows, cols), f32),
            pltpu.VMEM((rows, cols), f32),
            pltpu.VMEM((rows, cols), f32),
            pltpu.VMEM((2, 8, cols), f32),
            pltpu.VMEM((2, 8, cols), f32),
            pltpu.VMEM((2, rows, LANES), f32),
            pltpu.VMEM((2, rows, LANES), f32),
            dma(blocks + 2),
            *[pltpu.SemaphoreType.DMA((2, n))] * 8,
            dma(sht), dma(sht), dma(sht), dma(sht), dma(8), dma(8),
        ],
        compiler_params=pltpu.CompilerParams(
            collective_id=0, has_side_effects=True, vmem_limit_bytes=60 * 1024 * 1024
        ),
    )(
        height, east, north, depth, equilibrium, mask, sines[:, None], own_love, legendre,
        jnp.asarray(high), jnp.asarray(low),
    )


def solution(mesh):
    grid = P("ocean", "sht")
    in_specs = (grid,) * 6 + (P("ocean"), P("ocean", None, "sht"), P())
    return jax.shard_map(
        per_device, mesh=mesh, in_specs=in_specs, out_specs=(grid,) * 3, check_vma=False
    )
```
